256 devices in a mesh: tile: 16 (over z, x_hi), slab: 16 (over x_lo, y, core).
Axes of the slice: x: 4 (x_hi: 2, x_lo: 2; x = x_hi * 2 + x_lo), y: 4, z: 8, core: 2. Of those that a mesh axis runs over, the one named last changes fastest.
Arguments:
- start_volt: float32 [2, 128, 512, 2048], P(None, 'slab', 'tile'), may hold values from -6 to 6
- cap_rate: float32 [2, 512, 2048], P(None, 'tile'), may hold values from 0.2 to 0.6
- horiz_cond: float32 [2, 512, 2048], P(None, 'tile'), may hold values from 0.6 to 1.8
- vert_cond: float32 [2, 512, 2048], P(None, 'tile'), may hold values from 0.2 to 0.6
- via_cond: float32 [512, 2048], P('tile'), may hold values from 0.3 to 1
- line_inverse: float32 [2, 16, 128, 128], replicated, may hold values from 0 to 0.5
- cell_node: int32 [32768], P('tile'), may hold values from 0 to 65535
- cell_phase: int32 [32768], P('tile'), may hold values from 0 to 127
- cell_amp: float32 [32768], P('tile'), may hold values from 0.5 to 4
Outputs:
- voltage: float32 [2, 128, 512, 2048], P(None, 'slab', 'tile')
The draws below stay inside these ranges and needn't reach their ends.
Inputs may be any that keep to these rules, and one draw needn't show every extreme that they name: The cells of the t-th block of 2048 lie in tile t, and cell_node counts the nodes of that tile's 32 rows row by row from its first row.
All inputs are finite; a program needn't handle non-finite values.
Results may differ from the reference program's by a relative error of at most 0.00017.
Values sent between devices are 32-bit elements; how exact they have to be, the bound alone decides.
A program may use at most 128 MiB of HBM per device.

```python
import math
import jax
import jax.numpy as jnp
from jax import lax

ROWS_DEV = 32
COLS = 2048
CELLS_TILE = 2048
BLOCK = 128
PULSE = 4
ROWS = 512
PERIOD = 128
CELLS = 32768


def draw_line_inverse(key, part):
    key_factor = jax.random.fold_in(key, 11)
    key_scale = jax.random.fold_in(key, 23)
    offsets = jnp.arange(BLOCK)
    distance = jnp.abs(offsets[:, None] - offsets[None, :]).astype(jnp.float32)
    full_shape = (2, COLS // BLOCK, BLOCK, BLOCK)
    decay_ratio = 0.28
    diag_scale = 0.28
    factor = jax.random.uniform(key_factor, full_shape, jnp.float32, 0.75, 1.25)
    row_scale = jnp.exp(jax.random.uniform(key_scale, (2, COLS // BLOCK, BLOCK, 1), jnp.float32, -0.3, 0.3))
    return diag_scale * jnp.exp(distance * math.log(decay_ratio)) * factor * row_scale


def with_ends(drawn, own_key, low, high):
    shape = drawn.shape
    place = [jax.random.randint(jax.random.fold_in(own_key, axis), (), 0, shape[axis]) for axis in range(len(shape))]
    drawn = drawn.at[tuple(place)].set(low)
    longest = shape.index(max(shape))
    place[longest] = (place[longest] + 1) % shape[longest]
    return drawn.at[tuple(place)].set(high)


def shard_levels(key, extent, shards, least, top_value):
    def one(position, parts):
        steps = jax.random.uniform(jax.random.fold_in(jax.random.fold_in(key, 6), position), (parts,), jnp.float32, least / len(shards), top_value / len(shards))
        return jnp.repeat(jnp.exp(steps), extent[position] // parts).reshape((-1,) + (1,) * (len(extent) - position - 1))

    gain = one(*shards[0])
    for cut in shards[1:]:
        gain = gain * one(*cut)
    return gain


def scatter_about(stream_key, shape, deviation, limit, cuts=(), kind=jnp.bfloat16):
    entries = deviation * jax.random.normal(stream_key, shape, jnp.float32)
    if cuts:
        entries = entries * shard_levels(stream_key, shape, cuts, -0.22, 0.18)
    return jnp.clip(entries, -limit, limit).astype(kind)


def setup_inputs(seed: int = 0) -> dict:
    seeds = jax.random.split(jax.random.key(seed), 10)
    start_volt = scatter_about(seeds[0], (2, PERIOD, ROWS, COLS), 1.0, 6.0, ((1, 16), (2, 16)), jnp.float32)
    cap_rate = jnp.clip(jnp.exp(math.log(0.6) - 1.0986123 * jax.random.uniform(seeds[1], (2, ROWS, COLS), jnp.float32) ** shard_levels(seeds[1], (2, ROWS, COLS), ((1, 16),), -0.2, 0.2)), 0.2, 0.6)
    horiz_cond = jnp.clip(jnp.exp(math.log(1.8) - 1.0986122 * jax.random.uniform(seeds[2], (2, ROWS, COLS), jnp.float32) ** shard_levels(seeds[2], (2, ROWS, COLS), ((1, 16),), -0.2, 0.2)), 0.6, 1.8)
    vert_cond = jnp.clip(jnp.exp(math.log(0.6) - 1.0986123 * jax.random.uniform(seeds[3], (2, ROWS, COLS), jnp.float32) ** shard_levels(seeds[3], (2, ROWS, COLS), ((1, 16),), -0.2, 0.2)), 0.2, 0.6)
    via_cond = jnp.clip(jnp.exp(math.log(1.0) - 1.2039728 * jax.random.uniform(seeds[4], (ROWS, COLS), jnp.float32) ** shard_levels(seeds[4], (ROWS, COLS), ((0, 16),), -0.2, 0.2)), 0.3, 1.0)
    line_inverse = draw_line_inverse(jax.random.fold_in(seeds[9], 71), 0)
    cell_node = with_ends(jax.random.randint(seeds[6], (CELLS,), 0, ROWS_DEV * COLS), jax.random.fold_in(seeds[6], 1), 0, (ROWS_DEV * COLS) - 1).astype(jnp.int32)
    cell_phase = with_ends(jax.random.randint(seeds[7], (CELLS,), 0, PERIOD), jax.random.fold_in(seeds[7], 1), 0, PERIOD - 1).astype(jnp.int32)
    cell_amp = jnp.clip(jnp.exp(math.log(4.0) - 2.0794415 * jax.random.uniform(seeds[8], (CELLS,), jnp.float32) ** shard_levels(seeds[8], (CELLS,), ((0, 16),), -0.2, 0.2)), 0.5, 4.0)
    return dict(start_volt=start_volt, cap_rate=cap_rate, horiz_cond=horiz_cond, vert_cond=vert_cond, via_cond=via_cond, line_inverse=line_inverse, cell_node=cell_node, cell_phase=cell_phase, cell_amp=cell_amp)


def currents(cell_node, cell_phase, cell_amp):
    tile_of = jnp.arange(CELLS, dtype=jnp.int32) // CELLS_TILE
    node_ids = tile_of * (ROWS_DEV * COLS) + cell_node
    sample_ids = jnp.arange(PERIOD, dtype=jnp.int32)
    delay = jnp.mod(sample_ids[:, None] - cell_phase[None, :], PERIOD)
    weights = cell_amp[None, :] * jnp.where(delay < PULSE, (PULSE - delay).astype(jnp.float32) / PULSE, 0.0)
    injected = jnp.zeros((PERIOD, ROWS * COLS), jnp.float32).at[:, node_ids].add(weights)
    injected = injected.reshape(PERIOD, ROWS, COLS)
    return jnp.stack([injected, jnp.zeros_like(injected)])


def operate(voltage, cap_rate, horiz_cond, vert_cond, via_cond):
    before_one = jnp.roll(voltage, 1, axis=1)
    before_two = jnp.roll(voltage, 2, axis=1)
    capacitive = cap_rate[:, None] * (1.5 * voltage - 2.0 * before_one + 0.5 * before_two)
    padded = jnp.pad(voltage, ((0, 0), (0, 0), (0, 0), (1, 1)))
    horiz_flow = horiz_cond[:, None] * (2.0 * voltage - padded[..., :-2] - padded[..., 2:])
    padded = jnp.pad(voltage, ((0, 0), (0, 0), (1, 1), (0, 0)))
    vert_flow = vert_cond[:, None] * (2.0 * voltage - padded[:, :, :-2] - padded[:, :, 2:])
    via_flow = via_cond[None, None] * (voltage - voltage[::-1])
    return capacitive + horiz_flow + vert_flow + via_flow


def correct(resid, line_inverse):
    layers, sample_count, row_count, col_count = resid.shape
    pieces = resid.reshape(layers, sample_count, row_count, line_inverse.shape[1], line_inverse.shape[2])
    correction = jnp.einsum("ltrbj,lbij->ltrbi", pieces, line_inverse, precision=lax.Precision.HIGHEST)
    return correction.reshape(resid.shape)


def reference(start_volt, cap_rate, horiz_cond, vert_cond, via_cond, line_inverse, cell_node, cell_phase, cell_amp):
    right_side = currents(cell_node, cell_phase, cell_amp)
    voltage = start_volt
    for sweep_index in range(2):
        resid = right_side - operate(voltage, cap_rate, horiz_cond, vert_cond, via_cond)
        voltage = voltage + correct(resid, line_inverse)
    return voltage
```

```python
import functools

import jax
import jax.numpy as jnp
from jax import lax
from jax.experimental import pallas as pl
from jax.experimental.pallas import tpu as pltpu
from jax.sharding import PartitionSpec as P

PULSE = 4
LANES = 128
TOP = 8
MESH_ID = pl.DeviceIdType.MESH
BF = jnp.bfloat16
F32 = jnp.float32


def split(value):
    high = value.astype(BF)
    low = (value - high.astype(F32)).astype(BF)
    return high, low


def body(
    tiles,
    slabs,
    volt_in,
    cap_in,
    horiz_in,
    vert_in,
    via_in,
    inverse_in,
    node_in,
    phase_in,
    amp_in,
    out,
    start,
    first,
    cap,
    horiz,
    vert,
    via,
    diag,
    inverse,
    weights,
    source,
    node,
    phase,
    amp,
    column,
    spread,
    onehot,
    load_sem,
    block_sem,
    send_a,
    recv_a,
    send_b,
    recv_b,
    halo_send,
    halo_recv,
):
    samples, rows, cols = volt_in.shape[1], volt_in.shape[2], volt_in.shape[3]
    blocks = cols // LANES
    cells = node.shape[0] * LANES
    tile, slab = lax.axis_index("tile"), lax.axis_index("slab")
    ahead = (tile, lax.rem(slab + 1, slabs))
    behind = (tile, lax.rem(slab + slabs - 1, slabs))
    above, below = (tile - 1, slab), (tile + 1, slab)
    has_above, has_below = tile > 0, tile < tiles - 1
    body_rows = pl.ds(TOP, rows)

    barrier = pltpu.get_barrier_semaphore()
    pl.semaphore_signal(barrier, inc=1, device_id=ahead, device_id_type=MESH_ID)
    pl.semaphore_signal(barrier, inc=1, device_id=behind, device_id_type=MESH_ID)

    @pl.when(has_above)
    def _():
        pl.semaphore_signal(barrier, inc=1, device_id=above, device_id_type=MESH_ID)

    @pl.when(has_below)
    def _():
        pl.semaphore_signal(barrier, inc=1, device_id=below, device_id_type=MESH_ID)

    small = [
        pltpu.make_async_copy(one, other, load_sem.at[i])
        for i, (one, other) in enumerate(
            [
                (node_in, node),
                (phase_in, phase),
                (amp_in, amp),
                (inverse_in, inverse),
                (cap_in, cap),
                (horiz_in, horiz),
                (vert_in, vert),
                (via_in, via),
            ]
        )
    ]

    def load_block(b):
        return pltpu.make_async_copy(
            volt_in.at[:, :, :, pl.ds(pl.multiple_of(b * LANES, LANES), LANES)],
            start.at[:, pl.ds(2, samples), b + 1, body_rows, :],
            block_sem.at[b],
        )

    for copy in small[:3]:
        copy.start()

    @pl.loop(0, blocks)
    def _(b):
        load_block(b).start()

    for copy in small[3:]:
        copy.start()

    pl.semaphore_wait(barrier, 2 + has_above.astype(jnp.int32) + has_below.astype(jnp.int32))

    def send_start(b):
        return pltpu.make_async_remote_copy(
            src_ref=volt_in.at[
                :, pl.ds(samples - 2, 2), :, pl.ds(pl.multiple_of(b * LANES, LANES), LANES)
            ],
            dst_ref=start.at[:, pl.ds(0, 2), b + 1, body_rows, :],
            send_sem=send_a.at[b],
            recv_sem=recv_a.at[b],
            device_id=ahead,
            device_id_type=MESH_ID,
        )

    def send_first(b):
        return pltpu.make_async_remote_copy(
            src_ref=first.at[:, pl.ds(samples, 2), b + 1, body_rows, :],
            dst_ref=first.at[:, pl.ds(0, 2), b + 1, body_rows, :],
            send_sem=send_b.at[b],
            recv_sem=recv_b.at[b],
            device_id=ahead,
            device_id_type=MESH_ID,
        )

    def halo_copies(volt, low, count, slot):
        def one(row, to, device, sem):
            return pltpu.make_async_remote_copy(
                src_ref=volt.at[:, pl.ds(low + 2, count), pl.ds(1, blocks), pl.ds(row, 1), :],
                dst_ref=volt.at[:, pl.ds(low + 2, count), pl.ds(1, blocks), pl.ds(to, 1), :],
                send_sem=halo_send.at[sem],
                recv_sem=halo_recv.at[sem],
                device_id=device,
                device_id_type=MESH_ID,
            )

        up = one(TOP, TOP + rows, above, 2 * slot)
        down = one(TOP + rows - 1, TOP - 1, below, 2 * slot + 1)
        return up, down

    def send_halo(*what):
        up, down = halo_copies(*what)

        @pl.when(has_above)
        def _():
            up.start()

        @pl.when(has_below)
        def _():
            down.start()

    def wait_halo(*what):
        up, down = halo_copies(*what)

        @pl.when(has_below)
        def _():
            up.wait_recv()

        @pl.when(has_above)
        def _():
            down.wait_recv()

    def wait_halo_sent(*what):
        up, down = halo_copies(*what)

        @pl.when(has_above)
        def _():
            up.wait_send()

        @pl.when(has_below)
        def _():
            down.wait_send()

    @pl.loop(0, blocks)
    def _(b):
        send_start(b).start()

    @pl.loop(0, blocks)
    def _(b):
        load_block(b).wait()

    send_halo(start, 0, samples, 0)

    for volt in (start, first):
        for edge in (0, blocks + 1):
            volt[:, 2:, edge, body_rows, :] = jnp.zeros((2, samples, rows, LANES), F32)

        @pl.when(jnp.logical_not(has_above))
        def _():
            volt[:, 2:, :, pl.ds(TOP - 1, 1), :] = jnp.zeros((2, samples, blocks + 2, 1, LANES), F32)

        @pl.when(jnp.logical_not(has_below))
        def _():
            volt[:, 2:, :, pl.ds(TOP + rows, 1), :] = jnp.zeros(
                (2, samples, blocks + 2, 1, LANES), F32
            )

    for copy in small[:3]:
        copy.wait()
    period = samples * slabs
    moments = slab * samples + lax.broadcasted_iota(jnp.int32, (samples, LANES), 0)
    row_ids = lax.broadcasted_iota(jnp.int32, (rows, LANES), 0)

    @pl.loop(0, cells // LANES)
    def _(k):
        nodes = node[pl.ds(k, 1), :]
        delay = moments - phase[pl.ds(k, 1), :]
        delay = jnp.where(delay < 0, delay + period, delay)
        weight = amp[pl.ds(k, 1), :] * jnp.where(
            delay < PULSE, (PULSE - delay).astype(F32) * (1.0 / PULSE), 0.0
        )
        high = weight.astype(BF).astype(F32)
        low = weight - high
        here = row_ids == lax.div(nodes, cols)
        place = pl.ds(pl.multiple_of(k * LANES, LANES), LANES)
        for s in range(samples):
            for part, value in ((0, high), (1, low)):
                spread[pl.ds((part * samples + s) * rows, rows), place] = jnp.where(
                    here, value[s : s + 1, :], 0.0
                ).astype(BF)
        x = lax.rem(nodes, cols).astype(F32)
        column[place, :] = jnp.broadcast_to(x, (LANES, LANES)).T

    wide = 2 * LANES
    lane_ids = lax.broadcasted_iota(jnp.int32, (1, LANES), 1).astype(F32)

    @pl.loop(0, blocks // 2)
    def _(pair):
        base = (pair * wide).astype(F32)
        for half in range(2):
            ids = lane_ids + (base + half * LANES)
            onehot[:, half * LANES : (half + 1) * LANES] = jnp.where(
                column[...] == ids, 1.0, 0.0
            ).astype(BF)
        total = jnp.dot(spread[...], onehot[...], preferred_element_type=F32)
        total = total[: samples * rows] + total[samples * rows :]
        for half in range(2):
            source[:, pair * 2 + half] = total[:, half * LANES : (half + 1) * LANES].reshape(
                samples, rows, LANES
            )

    for copy in small[3:]:
        copy.wait()

    @pl.loop(0, blocks)
    def _(b):
        for l in range(2):
            high, low = split(inverse[l, b].T)
            both = jnp.concatenate([high, low], axis=1)
            weights[l, b] = jnp.concatenate([both, both], axis=0)

    diag[...] = (1.5 * cap[...] + 2.0 * horiz[...]) + (2.0 * vert[...] + via[...][None])

    lanes = lax.broadcasted_iota(jnp.int32, (16, LANES), 1)
    is_first, is_last = lanes == 0, lanes == LANES - 1

    def sweep_block(volt, b, low, count):
        place = pl.ds(pl.multiple_of(b * LANES, LANES), LANES)
        highs = {}
        for h in range(rows // 16):
            strip = pl.ds(16 * h, 16)
            coef = [
                [ref[l, strip, place] for ref in (cap, horiz, vert, diag)] for l in range(2)
            ]
            via_h = via[strip, place]

            def load(l, s, shift=0, side=0):
                return volt[l, s + 2, b + 1 + side, pl.ds(TOP + 16 * h + shift, 16), :]

            for s in range(low, low + count):
                centre = [load(l, s) for l in range(2)]
                for l in range(2):
                    cap_h, horiz_h, vert_h, diag_h = coef[l]
                    mid = centre[l]
                    left = pltpu.roll(jnp.where(is_last, load(l, s, 0, -1), mid), 1, 1)
                    right = pltpu.roll(jnp.where(is_first, load(l, s, 0, 1), mid), LANES - 1, 1)
                    resid = (
                        cap_h * (2.0 * load(l, s - 1) - 0.5 * load(l, s - 2))
                        + horiz_h * (left + right)
                        + vert_h * (load(l, s, -1) + load(l, s, 1))
                        + (via_h * centre[1 - l] - diag_h * mid)
                    )
                    if l == 0:
                        resid = resid + source[s, b, strip, :]
                    highs[l, s, h] = split(resid)
        new = []
        for l in range(2):
            order = [(s, h) for s in range(low, low + count) for h in range(rows // 16)]
            left_side = jnp.concatenate(
                [
                    jnp.concatenate([highs[l, s, h][part] for s, h in order], axis=0)
                    for part in range(2)
                ],
                axis=1,
            )
            product = jnp.dot(left_side, weights[l, b], preferred_element_type=F32)
            change = (product[:, :LANES] + product[:, LANES:]).reshape(count, rows, LANES)
            new.append(volt[l, pl.ds(low + 2, count), b + 1, body_rows, :] + change)
        return new

    def first_sweep(low, count, unroll, before=None, after=None):
        @pl.loop(0, blocks // unroll)
        def _(i):
            for j in range(unroll):
                b = i * unroll + j
                if before is not None:
                    before(b)
                new = sweep_block(start, b, low, count)
                for l in range(2):
                    first[l, pl.ds(low + 2, count), b + 1, body_rows, :] = new[l]
                if after is not None:
                    after(b)

    def second_sweep(low, count, unroll, before=None):
        @pl.loop(0, blocks // unroll)
        def _(i):
            for j in range(unroll):
                b = i * unroll + j
                if before is not None:
                    before(b)
                new = sweep_block(first, b, low, count)
                place = pl.ds(pl.multiple_of(b * LANES, LANES), LANES)
                for l in range(2):
                    out[l, pl.ds(low, count), :, place] = new[l]

    last, middle = (samples - 2, 2), (2, samples - 4)
    wait_halo(start, 0, samples, 0)
    first_sweep(*last, 1, after=lambda b: send_first(b).start())
    send_halo(first, *last, 1)
    first_sweep(*middle, 1)
    send_halo(first, *middle, 2)
    first_sweep(0, 2, 1, before=lambda b: send_start(b).wait_recv())
    send_halo(first, 0, 2, 3)
    wait_halo(first, *last, 1)
    wait_halo(first, *middle, 2)
    second_sweep(2, samples - 2, 1)
    wait_halo(first, 0, 2, 3)
    second_sweep(0, 2, 1, before=lambda b: send_first(b).wait_recv())

    @pl.loop(0, blocks)
    def _(b):
        send_start(b).wait_send()
        send_first(b).wait_send()

    wait_halo_sent(start, 0, samples, 0)
    wait_halo_sent(first, *last, 1)
    wait_halo_sent(first, *middle, 2)
    wait_halo_sent(first, 0, 2, 3)


def on_device(
    tiles,
    slabs,
    start_volt,
    cap_rate,
    horiz_cond,
    vert_cond,
    via_cond,
    line_inverse,
    cell_node,
    cell_phase,
    cell_amp,
):
    _, samples, rows, cols = start_volt.shape
    blocks = cols // LANES
    cells = cell_node.shape[0]
    grid = (2, samples + 2, blocks + 2, rows + 2 * TOP, LANES)
    dma = pltpu.SemaphoreType.DMA
    chunks = (cells // LANES, LANES)
    return pl.pallas_call(
        functools.partial(body, tiles, slabs),
        out_shape=jax.ShapeDtypeStruct(start_volt.shape, F32),
        in_specs=[pl.BlockSpec(memory_space=pl.ANY)] * 9,
        out_specs=pl.BlockSpec(memory_space=pltpu.VMEM),
        scratch_shapes=[
            pltpu.VMEM(grid, F32),
            pltpu.VMEM(grid, F32),
            pltpu.VMEM(cap_rate.shape, F32),
            pltpu.VMEM(cap_rate.shape, F32),
            pltpu.VMEM(cap_rate.shape, F32),
            pltpu.VMEM(via_cond.shape, F32),
            pltpu.VMEM(cap_rate.shape, F32),
            pltpu.VMEM(line_inverse.shape, F32),
            pltpu.VMEM((2, blocks, 2 * LANES, 2 * LANES), BF),
            pltpu.VMEM((samples, blocks, rows, LANES), F32),
            pltpu.VMEM(chunks, jnp.int32),
            pltpu.VMEM(chunks, jnp.int32),
            pltpu.VMEM(chunks, F32),
            pltpu.VMEM((cells, LANES), F32),
            pltpu.VMEM((2 * samples * rows, cells), BF),
            pltpu.VMEM((cells, 2 * LANES), BF),
            dma((8,)),
            dma((blocks,)),
            dma((blocks,)),
            dma((blocks,)),
            dma((blocks,)),
            dma((blocks,)),
            dma((8,)),
            dma((8,)),
        ],
        compiler_params=pltpu.CompilerParams(
            collective_id=0, has_side_effects=True, vmem_limit_bytes=58 * 1024 * 1024
        ),
    )(
        start_volt,
        cap_rate,
        horiz_cond,
        vert_cond,
        via_cond,
        line_inverse,
        cell_node.reshape(chunks),
        cell_phase.reshape(chunks),
        cell_amp.reshape(chunks),
    )


def solution(mesh):
    in_specs = (
        P(None, "slab", "tile", None),
        P(None, "tile", None),
        P(None, "tile", None),
        P(None, "tile", None),
        P("tile", None),
        P(),
        P("tile"),
        P("tile"),
        P("tile"),
    )
    out_specs = P(None, "slab", "tile", None)
    return jax.shard_map(
        functools.partial(on_device, mesh.shape["tile"], mesh.shape["slab"]),
        mesh=mesh,
        in_specs=in_specs,
        out_specs=out_specs,
        check_vma=False,
    )
```

```python
import functools

import jax
import jax.numpy as jnp
from jax import lax
from jax.experimental import pallas as pl
from jax.experimental.pallas import tpu as pltpu
from jax.sharding import PartitionSpec as P

PULSE = 4
LANES = 128
TOP = 8
MESH_ID = pl.DeviceIdType.MESH
BF = jnp.bfloat16
F32 = jnp.float32


def split(value):
    high = value.astype(BF)
    low = (value - high.astype(F32)).astype(BF)
    return high, low


def body(
    tiles,
    slabs,
    volt_in,
    cap_in,
    horiz_in,
    vert_in,
    via_in,
    inverse_in,
    node_in,
    phase_in,
    amp_in,
    out,
    start,
    first,
    cap,
    horiz,
    vert,
    via,
    diag,
    inverse,
    weights,
    source,
    node,
    phase,
    amp,
    column,
    spread,
    load_sem,
    block_sem,
    send_a,
    recv_a,
    send_b,
    recv_b,
    halo_send,
    halo_recv,
    relayed,
    relay_send,
    relay_recv,
):
    samples, rows, cols = volt_in.shape[1], volt_in.shape[2], volt_in.shape[3]
    blocks = cols // LANES
    cells = node.shape[0] * LANES
    tile, slab = lax.axis_index("tile"), lax.axis_index("slab")
    ahead = (tile, lax.rem(slab + 1, slabs))
    behind = (tile, lax.rem(slab + slabs - 1, slabs))
    above, below = (tile - 1, slab), (tile + 1, slab)
    has_above, has_below = tile > 0, tile < tiles - 1
    body_rows = pl.ds(TOP, rows)

    half = slabs // 2
    has_relay = half > 2
    place = lax.rem(slab, half)
    is_source, is_relay, is_target = place == half - 1, place == 1, place == 0
    relay = (tile, slab - (half - 2))
    relay_source = (tile, slab + (half - 2))
    relay_target = (tile, lax.rem(slab - 1 + half, slabs))
    target_relay = (tile, lax.rem(slab + 1 + half, slabs))

    barrier = pltpu.get_barrier_semaphore()

    def greet(device):
        pl.semaphore_signal(barrier, inc=1, device_id=device, device_id_type=MESH_ID)

    greet(behind)
    pl.when(has_above)(lambda: greet(above))
    pl.when(has_below)(lambda: greet(below))
    peers = 1 + has_above.astype(jnp.int32) + has_below.astype(jnp.int32)
    if has_relay:
        pl.when(is_relay)(lambda: greet(relay_source))
        pl.when(is_target)(lambda: greet(target_relay))
        peers = peers + (is_source | is_relay).astype(jnp.int32)

    small = [
        pltpu.make_async_copy(one, other, load_sem.at[i])
        for i, (one, other) in enumerate(
            [
                (node_in, node),
                (phase_in, phase),
                (amp_in, amp),
                (inverse_in, inverse),
                (cap_in, cap),
                (horiz_in, horiz),
                (vert_in, vert),
                (via_in, via),
            ]
        )
    ]

    def load_block(b):
        return pltpu.make_async_copy(
            volt_in.at[:, :, :, pl.ds(pl.multiple_of(b * LANES, LANES), LANES)],
            start.at[:, pl.ds(2, samples), b + 1, body_rows, :],
            block_sem.at[b],
        )

    for copy in small[:3]:
        copy.start()

    @pl.loop(0, blocks)
    def _(b):
        load_block(b).start()

    for copy in small[3:]:
        copy.start()

    for volt in (start, first):
        for edge in (0, blocks + 1):
            volt[:, 2:, edge, body_rows, :] = jnp.zeros((2, samples, rows, LANES), F32)

        @pl.when(jnp.logical_not(has_above))
        def _():
            volt[:, 2:, :, pl.ds(TOP - 1, 1), :] = jnp.zeros((2, samples, blocks + 2, 1, LANES), F32)

        @pl.when(jnp.logical_not(has_below))
        def _():
            volt[:, 2:, :, pl.ds(TOP + rows, 1), :] = jnp.zeros(
                (2, samples, blocks + 2, 1, LANES), F32
            )

    class Exchange:
        def __init__(self, volt, leaving, send_sem, recv_sem, number):
            self.volt, self.leaving, self.number = volt, leaving, number
            self.send_sem, self.recv_sem = send_sem, recv_sem

        def landing(self, b):
            return self.volt.at[:, pl.ds(0, 2), b + 1, body_rows, :]

        def direct(self, b):
            return pltpu.make_async_remote_copy(
                src_ref=self.leaving(b),
                dst_ref=self.landing(b),
                send_sem=self.send_sem.at[b],
                recv_sem=self.recv_sem.at[b],
                device_id=ahead,
                device_id_type=MESH_ID,
            )

        def to_relay(self, b):
            slot = self.number * (blocks // 2) + b // 2
            return pltpu.make_async_remote_copy(
                src_ref=self.leaving(b),
                dst_ref=relayed.at[slot],
                send_sem=self.send_sem.at[b],
                recv_sem=relay_recv.at[slot],
                device_id=relay,
                device_id_type=MESH_ID,
            )

        def onward(self, b):
            slot = self.number * (blocks // 2) + b // 2
            return pltpu.make_async_remote_copy(
                src_ref=relayed.at[slot],
                dst_ref=self.landing(b),
                send_sem=relay_send.at[slot],
                recv_sem=self.recv_sem.at[b],
                device_id=relay_target,
                device_id_type=MESH_ID,
            )

        def send_pair(self, b):
            self.direct(b).start()
            if has_relay:
                pl.when(is_source)(lambda: self.to_relay(b + 1).start())
                pl.when(jnp.logical_not(is_source))(lambda: self.direct(b + 1).start())
            else:
                self.direct(b + 1).start()

        def wait(self, b):
            self.direct(b).wait_recv()

        def wait_sent(self, b):
            self.direct(b).wait_send()

        def forward(self, k):
            if has_relay:

                @pl.when(is_relay)
                def _():
                    b = 2 * k + 1
                    self.to_relay(b).wait_recv()
                    self.onward(b).start()

        def wait_forwarded(self, k):
            if has_relay:

                @pl.when(is_relay)
                def _():
                    self.onward(2 * k + 1).wait_send()

    def start_leaving(b):
        lanes_b = pl.ds(pl.multiple_of(b * LANES, LANES), LANES)
        return volt_in.at[:, pl.ds(samples - 2, 2), :, lanes_b]

    def first_leaving(b):
        return first.at[:, pl.ds(samples, 2), b + 1, body_rows, :]

    before_one = Exchange(start, start_leaving, send_a, recv_a, 0)
    before_two = Exchange(first, first_leaving, send_b, recv_b, 1)

    def halo_copies(volt, low, count, slot):
        def one(row, to, device, sem):
            return pltpu.make_async_remote_copy(
                src_ref=volt.at[:, pl.ds(low + 2, count), pl.ds(1, blocks), pl.ds(row, 1), :],
                dst_ref=volt.at[:, pl.ds(low + 2, count), pl.ds(1, blocks), pl.ds(to, 1), :],
                send_sem=halo_send.at[sem],
                recv_sem=halo_recv.at[sem],
                device_id=device,
                device_id_type=MESH_ID,
            )

        up = one(TOP, TOP + rows, above, 2 * slot)
        down = one(TOP + rows - 1, TOP - 1, below, 2 * slot + 1)
        return up, down

    def send_halo(*what):
        up, down = halo_copies(*what)

        @pl.when(has_above)
        def _():
            up.start()

        @pl.when(has_below)
        def _():
            down.start()

    def wait_halo(*what):
        up, down = halo_copies(*what)

        @pl.when(has_below)
        def _():
            up.wait_recv()

        @pl.when(has_above)
        def _():
            down.wait_recv()

    def wait_halo_sent(*what):
        up, down = halo_copies(*what)

        @pl.when(has_above)
        def _():
            up.wait_send()

        @pl.when(has_below)
        def _():
            down.wait_send()

    pl.semaphore_wait(barrier, peers)

    @pl.loop(0, blocks // 2)
    def _(k):
        before_one.send_pair(2 * k)

    for copy in small[:3]:
        copy.wait()
    period = samples * slabs
    moments = slab * samples + lax.broadcasted_iota(jnp.int32, (samples, LANES), 0)
    row_ids = lax.broadcasted_iota(jnp.int32, (rows, LANES), 0)

    @pl.loop(0, cells // LANES)
    def _(k):
        nodes = node[pl.ds(k, 1), :]
        delay = moments - phase[pl.ds(k, 1), :]
        delay = jnp.where(delay < 0, delay + period, delay)
        weight = amp[pl.ds(k, 1), :] * jnp.where(
            delay < PULSE, (PULSE - delay).astype(F32) * (1.0 / PULSE), 0.0
        )
        high = weight.astype(BF).astype(F32)
        low = weight - high
        here = row_ids == lax.div(nodes, cols)
        place = pl.ds(pl.multiple_of(k * LANES, LANES), LANES)
        for s in range(samples):
            for part, value in ((0, high), (1, low)):
                spread[pl.ds((part * samples + s) * rows, rows), place] = jnp.where(
                    here, value[s : s + 1, :], 0.0
                ).astype(BF)
        x = lax.rem(nodes, cols).astype(F32)
        column[place, :] = jnp.broadcast_to(x, (LANES, LANES)).T

    wide = 2 * LANES
    lane_ids = lax.broadcasted_iota(jnp.int32, (1, LANES), 1).astype(F32)

    quads = blocks // 4

    @pl.loop(0, quads)
    def _(quad):
        for j in range(2):
            pair = quad * 2 + j
            base = (pair * wide).astype(F32)
            hot = jnp.concatenate(
                [
                    jnp.where(column[...] == lane_ids + (base + side * LANES), 1.0, 0.0).astype(BF)
                    for side in range(2)
                ],
                axis=1,
            )
            total = jnp.dot(spread[...], hot, preferred_element_type=F32)
            total = total[: samples * rows] + total[samples * rows :]
            for side in range(2):
                source[:, pair * 2 + side] = total[:, side * LANES : (side + 1) * LANES].reshape(
                    samples, rows, LANES
                )

        @pl.when(quad == 0)
        def _():
            @pl.loop(0, blocks)
            def _(b):
                load_block(b).wait()

            send_halo(start, 0, samples, 0)

        @pl.when(quad > 0)
        def _():
            before_one.forward(quad - 1)

    before_one.forward(quads - 1)

    for copy in small[3:]:
        copy.wait()

    @pl.loop(0, blocks)
    def _(b):
        for l in range(2):
            high, low = split(inverse[l, b])
            both = jnp.concatenate([high, low], axis=0)
            weights[l, b] = jnp.concatenate([both, both], axis=1)

    diag[...] = (1.5 * cap[...] + 2.0 * horiz[...]) + (2.0 * vert[...] + via[...][None])

    lanes = lax.broadcasted_iota(jnp.int32, (16, LANES), 1)
    is_first, is_last = lanes == 0, lanes == LANES - 1

    def sweep_block(volt, b, low, count):
        place = pl.ds(pl.multiple_of(b * LANES, LANES), LANES)
        highs = {}
        for h in range(rows // 16):
            strip = pl.ds(16 * h, 16)
            coef = [
                [ref[l, strip, place] for ref in (cap, horiz, vert, diag)] for l in range(2)
            ]
            via_h = via[strip, place]

            def load(l, s, shift=0, side=0):
                return volt[l, s + 2, b + 1 + side, pl.ds(TOP + 16 * h + shift, 16), :]

            for s in range(low, low + count):
                centre = [load(l, s) for l in range(2)]
                for l in range(2):
                    cap_h, horiz_h, vert_h, diag_h = coef[l]
                    mid = centre[l]
                    left = pltpu.roll(jnp.where(is_last, load(l, s, 0, -1), mid), 1, 1)
                    right = pltpu.roll(jnp.where(is_first, load(l, s, 0, 1), mid), LANES - 1, 1)
                    resid = (
                        cap_h * (2.0 * load(l, s - 1) - 0.5 * load(l, s - 2))
                        + horiz_h * (left + right)
                        + vert_h * (load(l, s, -1) + load(l, s, 1))
                        + (via_h * centre[1 - l] - diag_h * mid)
                    )
                    if l == 0:
                        resid = resid + source[s, b, strip, :]
                    highs[l, s, h] = split(resid)
        new = []
        for l in range(2):
            order = [(s, h) for s in range(low, low + count) for h in range(rows // 16)]
            left_side = jnp.concatenate(
                [
                    jnp.concatenate([highs[l, s, h][part] for s, h in order], axis=0)
                    for part in range(2)
                ],
                axis=1,
            )
            product = lax.dot_general(
                left_side, weights[l, b], (((1,), (1,)), ((), ())), preferred_element_type=F32
            )
            change = (product[:, :LANES] + product[:, LANES:]).reshape(count, rows, LANES)
            new.append(volt[l, pl.ds(low + 2, count), b + 1, body_rows, :] + change)
        return new

    unroll = 4
    turns = blocks // unroll

    def sweep(volt, low, count, store, before=None, after=None):
        @pl.loop(0, turns)
        def _(i):
            taken = [i * unroll + j for j in range(unroll)]
            if before is not None:
                for b in taken:
                    before(b)
            for b in taken:
                store(b, low, count, sweep_block(volt, b, low, count))
            if after is not None:
                after(i)

    def to_first(b, low, count, new):
        for l in range(2):
            first[l, pl.ds(low + 2, count), b + 1, body_rows, :] = new[l]

    def to_out(b, low, count, new):
        lanes_b = pl.ds(pl.multiple_of(b * LANES, LANES), LANES)
        for l in range(2):
            out[l, pl.ds(low, count), :, lanes_b] = new[l]

    def send_turn(i):
        for j in range(0, unroll, 2):
            before_two.send_pair(i * unroll + j)

    def forwards(exchange, shift, turn):
        def after(i):
            pl.when(lax.rem(i, turn) == turn - 1)(
                lambda: exchange.forward(shift + lax.div(i, turn))
            )

        return after

    relays = blocks // 2
    last, middle = (samples - 2, 2), (2, samples - 4)
    wait_halo(start, 0, samples, 0)
    sweep(start, *last, to_first, after=send_turn)
    send_halo(first, *last, 1)
    sweep(start, *middle, to_first, after=forwards(before_one, quads, 2))
    send_halo(first, *middle, 2)

    @pl.loop(quads + turns // 2, relays)
    def _(k):
        before_one.forward(k)

    sweep(start, 0, 2, to_first, before=before_one.wait)
    send_halo(first, 0, 2, 3)
    wait_halo(first, *last, 1)
    wait_halo(first, *middle, 2)
    sweep(first, 2, samples - 2, to_out, after=forwards(before_two, 0, 1))
    wait_halo(first, 0, 2, 3)
    sweep(first, 0, 2, to_out, before=before_two.wait)

    @pl.loop(turns, relays)
    def _(k):
        before_two.forward(k)

    @pl.loop(0, blocks)
    def _(b):
        before_one.wait_sent(b)
        before_two.wait_sent(b)

    @pl.loop(0, relays)
    def _(k):
        before_one.wait_forwarded(k)
        before_two.wait_forwarded(k)

    wait_halo_sent(start, 0, samples, 0)
    wait_halo_sent(first, *last, 1)
    wait_halo_sent(first, *middle, 2)
    wait_halo_sent(first, 0, 2, 3)


def on_device(
    tiles,
    slabs,
    start_volt,
    cap_rate,
    horiz_cond,
    vert_cond,
    via_cond,
    line_inverse,
    cell_node,
    cell_phase,
    cell_amp,
):
    _, samples, rows, cols = start_volt.shape
    blocks = cols // LANES
    cells = cell_node.shape[0]
    grid = (2, samples + 2, blocks + 2, rows + 2 * TOP, LANES)
    dma = pltpu.SemaphoreType.DMA
    chunks = (cells // LANES, LANES)
    return pl.pallas_call(
        functools.partial(body, tiles, slabs),
        out_shape=pltpu.VMEM(start_volt.shape, F32),
        in_specs=[pl.BlockSpec(memory_space=pltpu.HBM)] * 9,
        out_specs=pl.BlockSpec(memory_space=pltpu.VMEM),
        scratch_shapes=[
            pltpu.VMEM(grid, F32),
            pltpu.VMEM(grid, F32),
            pltpu.VMEM(cap_rate.shape, F32),
            pltpu.VMEM(cap_rate.shape, F32),
            pltpu.VMEM(cap_rate.shape, F32),
            pltpu.VMEM(via_cond.shape, F32),
            pltpu.VMEM(cap_rate.shape, F32),
            pltpu.VMEM(line_inverse.shape, F32),
            pltpu.VMEM((2, blocks, 2 * LANES, 2 * LANES), BF),
            pltpu.VMEM((samples, blocks, rows, LANES), F32),
            pltpu.VMEM(chunks, jnp.int32),
            pltpu.VMEM(chunks, jnp.int32),
            pltpu.VMEM(chunks, F32),
            pltpu.VMEM((cells, LANES), F32),
            pltpu.VMEM((2 * samples * rows, cells), BF),
            dma((8,)),
            dma((blocks,)),
            dma((blocks,)),
            dma((blocks,)),
            dma((blocks,)),
            dma((blocks,)),
            dma((8,)),
            dma((8,)),
            pltpu.VMEM((blocks, 2, 2, rows, LANES), F32),
            dma((blocks,)),
            dma((blocks,)),
        ],
        compiler_params=pltpu.CompilerParams(
            collective_id=0, has_side_effects=True, vmem_limit_bytes=44 * 1024 * 1024
        ),
    )(
        *(
            pltpu.with_memory_space_constraint(value, pltpu.HBM)
            for value in (
                start_volt,
                cap_rate,
                horiz_cond,
                vert_cond,
                via_cond,
                line_inverse,
                cell_node.reshape(chunks),
                cell_phase.reshape(chunks),
                cell_amp.reshape(chunks),
            )
        )
    )


def solution(mesh):
    in_specs = (
        P(None, "slab", "tile", None),
        P(None, "tile", None),
        P(None, "tile", None),
        P(None, "tile", None),
        P("tile", None),
        P(),
        P("tile"),
        P("tile"),
        P("tile"),
    )
    out_specs = P(None, "slab", "tile", None)
    return jax.shard_map(
        functools.partial(on_device, mesh.shape["tile"], mesh.shape["slab"]),
        mesh=mesh,
        in_specs=in_specs,
        out_specs=out_specs,
        check_vma=False,
    )
```

```python
import functools

import jax
import jax.numpy as jnp
from jax import lax
from jax.experimental import pallas as pl
from jax.experimental.pallas import tpu as pltpu
from jax.sharding import PartitionSpec as P

PULSE = 4
LANES = 128
TOP = 8
MESH_ID = pl.DeviceIdType.MESH
BF = jnp.bfloat16
F32 = jnp.float32


def split(value):
    high = value.astype(BF)
    low = (value - high.astype(F32)).astype(BF)
    return high, low


def body(
    tiles,
    slabs,
    volt_in,
    cap_in,
    horiz_in,
    vert_in,
    via_in,
    inverse_in,
    node_in,
    phase_in,
    amp_in,
    out,
    start,
    first,
    cap,
    horiz,
    vert,
    via,
    diag,
    inverse,
    weights,
    source,
    node,
    phase,
    amp,
    column,
    spread,
    load_sem,
    block_sem,
    send_a,
    recv_a,
    send_b,
    recv_b,
    halo_send,
    halo_recv,
    relayed,
    relay_send,
    relay_recv,
):
    samples, rows, cols = volt_in.shape[1], volt_in.shape[2], volt_in.shape[3]
    blocks = cols // LANES
    cells = node.shape[0] * LANES
    tile, slab = lax.axis_index("tile"), lax.axis_index("slab")
    ahead = (tile, lax.rem(slab + 1, slabs))
    behind = (tile, lax.rem(slab + slabs - 1, slabs))
    above, below = (tile - 1, slab), (tile + 1, slab)
    has_above, has_below = tile > 0, tile < tiles - 1
    body_rows = pl.ds(TOP, rows)

    relays = blocks // 2
    half = slabs // 2
    has_relay = half > 1
    place = lax.rem(slab, half)
    is_source, is_relay = place == half - 1, place == 0
    relay = (tile, slab - (half - 1))
    relay_source = (tile, slab + (half - 1))
    relay_target = (tile, lax.rem(slab + half, slabs))

    barrier = pltpu.get_barrier_semaphore()

    def greet(device):
        pl.semaphore_signal(barrier, inc=1, device_id=device, device_id_type=MESH_ID)

    greet(behind)
    pl.when(has_above)(lambda: greet(above))
    pl.when(has_below)(lambda: greet(below))
    peers = 1 + has_above.astype(jnp.int32) + has_below.astype(jnp.int32)
    if has_relay:
        pl.when(is_relay)(lambda: greet(relay_source))
        pl.when(is_relay)(lambda: greet(relay_target))
        peers = peers + (is_source | is_relay).astype(jnp.int32)

    small = [
        pltpu.make_async_copy(one, other, load_sem.at[i])
        for i, (one, other) in enumerate(
            [
                (node_in, node),
                (phase_in, phase),
                (amp_in, amp),
                (inverse_in, inverse),
                (cap_in, cap),
                (horiz_in, horiz),
                (vert_in, vert),
                (via_in, via),
            ]
        )
    ]

    def load_block(b):
        return pltpu.make_async_copy(
            volt_in.at[:, :, :, pl.ds(pl.multiple_of(b * LANES, LANES), LANES)],
            start.at[:, pl.ds(2, samples), b + 1, body_rows, :],
            block_sem.at[b],
        )

    for copy in small[:3]:
        copy.start()

    @pl.loop(0, blocks)
    def _(b):
        load_block(b).start()

    for copy in small[3:]:
        copy.start()

    for volt in (start, first):
        for edge in (0, blocks + 1):
            volt[:, 2:, edge, body_rows, :] = jnp.zeros((2, samples, rows, LANES), F32)

        @pl.when(jnp.logical_not(has_above))
        def _():
            volt[:, 2:, :, pl.ds(TOP - 1, 1), :] = jnp.zeros((2, samples, blocks + 2, 1, LANES), F32)

        @pl.when(jnp.logical_not(has_below))
        def _():
            volt[:, 2:, :, pl.ds(TOP + rows, 1), :] = jnp.zeros(
                (2, samples, blocks + 2, 1, LANES), F32
            )

    class Exchange:
        def __init__(self, volt, leaving, send_sem, recv_sem, number):
            self.volt, self.leaving, self.number = volt, leaving, number
            self.send_sem, self.recv_sem = send_sem, recv_sem

        def landing(self, b):
            return self.volt.at[:, pl.ds(0, 2), b + 1, body_rows, :]

        def direct(self, b):
            return pltpu.make_async_remote_copy(
                src_ref=self.leaving(b),
                dst_ref=self.landing(b),
                send_sem=self.send_sem.at[b],
                recv_sem=self.recv_sem.at[b],
                device_id=ahead,
                device_id_type=MESH_ID,
            )

        def to_relay(self, b):
            slot = self.number * relays + b
            return pltpu.make_async_remote_copy(
                src_ref=self.leaving(b),
                dst_ref=relayed.at[slot],
                send_sem=self.send_sem.at[b],
                recv_sem=relay_recv.at[slot],
                device_id=relay,
                device_id_type=MESH_ID,
            )

        def onward(self, b):
            slot = self.number * relays + b
            return pltpu.make_async_remote_copy(
                src_ref=relayed.at[slot],
                dst_ref=self.landing(b),
                send_sem=relay_send.at[slot],
                recv_sem=self.recv_sem.at[b],
                device_id=relay_target,
                device_id_type=MESH_ID,
            )

        def send(self, b):
            if has_relay:
                goes_round = is_source & (b < relays)
                pl.when(goes_round)(lambda: self.to_relay(b).start())
                pl.when(jnp.logical_not(goes_round))(lambda: self.direct(b).start())
            else:
                self.direct(b).start()

        def wait(self, b):
            self.direct(b).wait_recv()

        def wait_sent(self, b):
            self.direct(b).wait_send()

        def forward(self, low, high):
            if has_relay:

                @pl.when(is_relay)
                def _():
                    @pl.loop(low, high)
                    def _(b):
                        self.to_relay(b).wait_recv()
                        self.onward(b).start()

        def wait_forwarded(self):
            if has_relay:

                @pl.when(is_relay)
                def _():
                    @pl.loop(0, relays)
                    def _(b):
                        self.onward(b).wait_send()

    def start_leaving(b):
        lanes_b = pl.ds(pl.multiple_of(b * LANES, LANES), LANES)
        return volt_in.at[:, pl.ds(samples - 2, 2), :, lanes_b]

    def first_leaving(b):
        return first.at[:, pl.ds(samples, 2), b + 1, body_rows, :]

    before_one = Exchange(start, start_leaving, send_a, recv_a, 0)
    before_two = Exchange(first, first_leaving, send_b, recv_b, 1)

    def halo_copies(volt, low, count, slot):
        def one(row, to, device, sem):
            return pltpu.make_async_remote_copy(
                src_ref=volt.at[:, pl.ds(low + 2, count), pl.ds(1, blocks), pl.ds(row, 1), :],
                dst_ref=volt.at[:, pl.ds(low + 2, count), pl.ds(1, blocks), pl.ds(to, 1), :],
                send_sem=halo_send.at[sem],
                recv_sem=halo_recv.at[sem],
                device_id=device,
                device_id_type=MESH_ID,
            )

        up = one(TOP, TOP + rows, above, 2 * slot)
        down = one(TOP + rows - 1, TOP - 1, below, 2 * slot + 1)
        return up, down

    def send_halo(*what):
        up, down = halo_copies(*what)

        @pl.when(has_above)
        def _():
            up.start()

        @pl.when(has_below)
        def _():
            down.start()

    def wait_halo(*what):
        up, down = halo_copies(*what)

        @pl.when(has_below)
        def _():
            up.wait_recv()

        @pl.when(has_above)
        def _():
            down.wait_recv()

    def wait_halo_sent(*what):
        up, down = halo_copies(*what)

        @pl.when(has_above)
        def _():
            up.wait_send()

        @pl.when(has_below)
        def _():
            down.wait_send()

    pl.semaphore_wait(barrier, peers)

    early = blocks // 4
    pl.loop(0, early)(before_one.send)

    for copy in small[:3]:
        copy.wait()
    period = samples * slabs
    moments = slab * samples + lax.broadcasted_iota(jnp.int32, (samples, LANES), 0)
    row_ids = lax.broadcasted_iota(jnp.int32, (rows, LANES), 0)

    @pl.loop(0, cells // LANES)
    def _(k):
        nodes = node[pl.ds(k, 1), :]
        delay = moments - phase[pl.ds(k, 1), :]
        delay = jnp.where(delay < 0, delay + period, delay)
        weight = amp[pl.ds(k, 1), :] * jnp.where(
            delay < PULSE, (PULSE - delay).astype(F32) * (1.0 / PULSE), 0.0
        )
        high = weight.astype(BF).astype(F32)
        low = weight - high
        here = row_ids == lax.div(nodes, cols)
        place = pl.ds(pl.multiple_of(k * LANES, LANES), LANES)
        for s in range(samples):
            for part, value in ((0, high), (1, low)):
                spread[pl.ds((part * samples + s) * rows, rows), place] = jnp.where(
                    here, value[s : s + 1, :], 0.0
                ).astype(BF)
        x = lax.rem(nodes, cols).astype(F32)
        column[place, :] = jnp.broadcast_to(x, (LANES, LANES)).T

    wide = 2 * LANES
    lane_ids = lax.broadcasted_iota(jnp.int32, (1, LANES), 1).astype(F32)

    quads = blocks // 4

    @pl.loop(0, quads)
    def _(quad):
        for j in range(2):
            pair = quad * 2 + j
            base = (pair * wide).astype(F32)
            hot = jnp.concatenate(
                [
                    jnp.where(column[...] == lane_ids + (base + side * LANES), 1.0, 0.0).astype(BF)
                    for side in range(2)
                ],
                axis=1,
            )
            total = jnp.dot(spread[...], hot, preferred_element_type=F32)
            total = total[: samples * rows] + total[samples * rows :]
            for side in range(2):
                source[:, pair * 2 + side] = total[:, side * LANES : (side + 1) * LANES].reshape(
                    samples, rows, LANES
                )

        @pl.when(quad == 0)
        def _():
            @pl.loop(0, blocks)
            def _(b):
                load_block(b).wait()

            send_halo(start, 0, samples, 0)
            pl.loop(early, blocks)(before_one.send)

        @pl.when(quad > 0)
        def _():
            before_one.forward(2 * quad - 2, 2 * quad)

    for copy in small[3:]:
        copy.wait()

    @pl.loop(0, blocks)
    def _(b):
        for l in range(2):
            high, low = split(inverse[l, b])
            both = jnp.concatenate([high, low], axis=0)
            weights[l, b] = jnp.concatenate([both, both], axis=1)

    diag[...] = (1.5 * cap[...] + 2.0 * horiz[...]) + (2.0 * vert[...] + via[...][None])

    lanes = lax.broadcasted_iota(jnp.int32, (16, LANES), 1)
    is_first, is_last = lanes == 0, lanes == LANES - 1

    def sweep_block(volt, b, low, count):
        place = pl.ds(pl.multiple_of(b * LANES, LANES), LANES)
        highs = {}
        for h in range(rows // 16):
            strip = pl.ds(16 * h, 16)
            coef = [
                [ref[l, strip, place] for ref in (cap, horiz, vert, diag)] for l in range(2)
            ]
            via_h = via[strip, place]

            def load(l, s, shift=0, side=0):
                return volt[l, s + 2, b + 1 + side, pl.ds(TOP + 16 * h + shift, 16), :]

            for s in range(low, low + count):
                centre = [load(l, s) for l in range(2)]
                for l in range(2):
                    cap_h, horiz_h, vert_h, diag_h = coef[l]
                    mid = centre[l]
                    left = pltpu.roll(jnp.where(is_last, load(l, s, 0, -1), mid), 1, 1)
                    right = pltpu.roll(jnp.where(is_first, load(l, s, 0, 1), mid), LANES - 1, 1)
                    resid = (
                        cap_h * (2.0 * load(l, s - 1) - 0.5 * load(l, s - 2))
                        + horiz_h * (left + right)
                        + vert_h * (load(l, s, -1) + load(l, s, 1))
                        + (via_h * centre[1 - l] - diag_h * mid)
                    )
                    if l == 0:
                        resid = resid + source[s, b, strip, :]
                    highs[l, s, h] = split(resid)
        new = []
        for l in range(2):
            order = [(s, h) for s in range(low, low + count) for h in range(rows // 16)]
            left_side = jnp.concatenate(
                [
                    jnp.concatenate([highs[l, s, h][part] for s, h in order], axis=0)
                    for part in range(2)
                ],
                axis=1,
            )
            product = lax.dot_general(
                left_side, weights[l, b], (((1,), (1,)), ((), ())), preferred_element_type=F32
            )
            change = (product[:, :LANES] + product[:, LANES:]).reshape(count, rows, LANES)
            new.append(volt[l, pl.ds(low + 2, count), b + 1, body_rows, :] + change)
        return new

    unroll = 4
    turns = blocks // unroll

    def sweep(volt, low, count, store, before=None, after=None):
        @pl.loop(0, turns)
        def _(i):
            taken = [i * unroll + j for j in range(unroll)]
            if before is not None:
                for b in taken:
                    before(b)
            for b in taken:
                store(b, low, count, sweep_block(volt, b, low, count))
            if after is not None:
                after(i)

    def to_first(b, low, count, new):
        for l in range(2):
            first[l, pl.ds(low + 2, count), b + 1, body_rows, :] = new[l]

    def to_out(b, low, count, new):
        lanes_b = pl.ds(pl.multiple_of(b * LANES, LANES), LANES)
        for l in range(2):
            out[l, pl.ds(low, count), :, lanes_b] = new[l]

    last, middle = (samples - 2, 2), (2, samples - 4)

    def send_range(low, high):
        pl.loop(low, high)(before_two.send)

    def after_middle(i):
        pl.when(i == 1)(lambda: send_range(2, 4))

    def after_inner(i):
        pl.when(i < 3)(lambda: before_two.forward(2 + 2 * i, jnp.minimum(4 + 2 * i, relays)))

    wait_halo(start, 0, samples, 0)
    sweep(start, *last, to_first)
    send_halo(first, *last, 1)
    send_range(0, 2)
    before_one.forward(2 * quads - 2, relays)
    sweep(start, *middle, to_first, after=after_middle)
    send_halo(first, *middle, 2)
    send_range(4, blocks // 2)
    sweep(start, 0, 2, to_first, before=before_one.wait)
    send_halo(first, 0, 2, 3)
    send_range(blocks // 2, blocks)
    before_two.forward(0, 2)
    wait_halo(first, *last, 1)
    wait_halo(first, *middle, 2)
    sweep(first, 2, samples - 2, to_out, after=after_inner)
    wait_halo(first, 0, 2, 3)
    sweep(first, 0, 2, to_out, before=before_two.wait)

    @pl.loop(0, blocks)
    def _(b):
        before_one.wait_sent(b)
        before_two.wait_sent(b)

    before_one.wait_forwarded()
    before_two.wait_forwarded()
    wait_halo_sent(start, 0, samples, 0)
    wait_halo_sent(first, *last, 1)
    wait_halo_sent(first, *middle, 2)
    wait_halo_sent(first, 0, 2, 3)


def on_device(
    tiles,
    slabs,
    start_volt,
    cap_rate,
    horiz_cond,
    vert_cond,
    via_cond,
    line_inverse,
    cell_node,
    cell_phase,
    cell_amp,
):
    _, samples, rows, cols = start_volt.shape
    blocks = cols // LANES
    cells = cell_node.shape[0]
    grid = (2, samples + 2, blocks + 2, rows + 2 * TOP, LANES)
    dma = pltpu.SemaphoreType.DMA
    chunks = (cells // LANES, LANES)
    return pl.pallas_call(
        functools.partial(body, tiles, slabs),
        out_shape=pltpu.VMEM(start_volt.shape, F32),
        in_specs=[pl.BlockSpec(memory_space=pltpu.HBM)] * 9,
        out_specs=pl.BlockSpec(memory_space=pltpu.VMEM),
        scratch_shapes=[
            pltpu.VMEM(grid, F32),
            pltpu.VMEM(grid, F32),
            pltpu.VMEM(cap_rate.shape, F32),
            pltpu.VMEM(cap_rate.shape, F32),
            pltpu.VMEM(cap_rate.shape, F32),
            pltpu.VMEM(via_cond.shape, F32),
            pltpu.VMEM(cap_rate.shape, F32),
            pltpu.VMEM(line_inverse.shape, F32),
            pltpu.VMEM((2, blocks, 2 * LANES, 2 * LANES), BF),
            pltpu.VMEM((samples, blocks, rows, LANES), F32),
            pltpu.VMEM(chunks, jnp.int32),
            pltpu.VMEM(chunks, jnp.int32),
            pltpu.VMEM(chunks, F32),
            pltpu.VMEM((cells, LANES), F32),
            pltpu.VMEM((2 * samples * rows, cells), BF),
            dma((8,)),
            dma((blocks,)),
            dma((blocks,)),
            dma((blocks,)),
            dma((blocks,)),
            dma((blocks,)),
            dma((8,)),
            dma((8,)),
            pltpu.VMEM((blocks, 2, 2, rows, LANES), F32),
            dma((blocks,)),
            dma((blocks,)),
        ],
        compiler_params=pltpu.CompilerParams(
            collective_id=0, has_side_effects=True, vmem_limit_bytes=44 * 1024 * 1024
        ),
    )(
        *(
            pltpu.with_memory_space_constraint(value, pltpu.HBM)
            for value in (
                start_volt,
                cap_rate,
                horiz_cond,
                vert_cond,
                via_cond,
                line_inverse,
                cell_node.reshape(chunks),
                cell_phase.reshape(chunks),
                cell_amp.reshape(chunks),
            )
        )
    )


def solution(mesh):
    in_specs = (
        P(None, "slab", "tile", None),
        P(None, "tile", None),
        P(None, "tile", None),
        P(None, "tile", None),
        P("tile", None),
        P(),
        P("tile"),
        P("tile"),
        P("tile"),
    )
    out_specs = P(None, "slab", "tile", None)
    return jax.shard_map(
        functools.partial(on_device, mesh.shape["tile"], mesh.shape["slab"]),
        mesh=mesh,
        in_specs=in_specs,
        out_specs=out_specs,
        check_vma=False,
    )
```

```python
import functools

import jax
import jax.numpy as jnp
from jax import lax
from jax.experimental import pallas as pl
from jax.experimental.pallas import tpu as pltpu
from jax.sharding import PartitionSpec as P

PULSE = 4
LANES = 128
TOP = 8
MESH_ID = pl.DeviceIdType.MESH
BF = jnp.bfloat16
F32 = jnp.float32


def split(value):
    high = value.astype(BF)
    low = (value - high.astype(F32)).astype(BF)
    return high, low


def body(
    tiles,
    slabs,
    volt_in,
    cap_in,
    horiz_in,
    vert_in,
    via_in,
    inverse_in,
    node_in,
    phase_in,
    amp_in,
    out,
    start,
    first,
    cap,
    horiz,
    vert,
    via,
    diag,
    inverse,
    weights,
    source,
    node,
    phase,
    amp,
    column,
    spread,
    load_sem,
    block_sem,
    send_a,
    recv_a,
    send_b,
    recv_b,
    halo_send,
    halo_recv,
    relayed,
    relay_send,
    relay_recv,
):
    samples, rows, cols = volt_in.shape[1], volt_in.shape[2], volt_in.shape[3]
    blocks = cols // LANES
    cells = node.shape[0] * LANES
    tile, slab = lax.axis_index("tile"), lax.axis_index("slab")
    ahead = (tile, lax.rem(slab + 1, slabs))
    behind = (tile, lax.rem(slab + slabs - 1, slabs))
    above, below = (tile - 1, slab), (tile + 1, slab)
    has_above, has_below = tile > 0, tile < tiles - 1
    body_rows = pl.ds(TOP, rows)

    relays = blocks // 2
    half = slabs // 2
    has_relay = half > 1
    place = lax.rem(slab, half)
    is_source, is_relay = place == half - 1, place == 0
    relay = (tile, slab - (half - 1))
    relay_source = (tile, slab + (half - 1))
    relay_target = (tile, lax.rem(slab + half, slabs))

    barrier = pltpu.get_barrier_semaphore()

    def greet(device):
        pl.semaphore_signal(barrier, inc=1, device_id=device, device_id_type=MESH_ID)

    greet(behind)
    pl.when(has_above)(lambda: greet(above))
    pl.when(has_below)(lambda: greet(below))
    peers = 1 + has_above.astype(jnp.int32) + has_below.astype(jnp.int32)
    if has_relay:
        pl.when(is_relay)(lambda: greet(relay_source))
        pl.when(is_relay)(lambda: greet(relay_target))
        peers = peers + (is_source | is_relay).astype(jnp.int32)

    small = [
        pltpu.make_async_copy(one, other, load_sem.at[i])
        for i, (one, other) in enumerate(
            [
                (node_in, node),
                (phase_in, phase),
                (amp_in, amp),
                (inverse_in, inverse),
                (cap_in, cap),
                (horiz_in, horiz),
                (vert_in, vert),
                (via_in, via),
            ]
        )
    ]

    def load_block(b):
        return pltpu.make_async_copy(
            volt_in.at[:, :, :, pl.ds(pl.multiple_of(b * LANES, LANES), LANES)],
            start.at[:, pl.ds(2, samples), b + 1, body_rows, :],
            block_sem.at[b],
        )

    for copy in small[:3]:
        copy.start()

    @pl.loop(0, blocks)
    def _(b):
        load_block(b).start()

    for copy in small[3:]:
        copy.start()

    for volt in (start, first):
        for edge in (0, blocks + 1):
            volt[:, 2:, edge, body_rows, :] = jnp.zeros((2, samples, rows, LANES), F32)

        @pl.when(jnp.logical_not(has_above))
        def _():
            volt[:, 2:, :, pl.ds(TOP - 1, 1), :] = jnp.zeros((2, samples, blocks + 2, 1, LANES), F32)

        @pl.when(jnp.logical_not(has_below))
        def _():
            volt[:, 2:, :, pl.ds(TOP + rows, 1), :] = jnp.zeros(
                (2, samples, blocks + 2, 1, LANES), F32
            )

    class Exchange:
        def __init__(self, volt, leaving, send_sem, recv_sem, number):
            self.volt, self.leaving, self.number = volt, leaving, number
            self.send_sem, self.recv_sem = send_sem, recv_sem

        def landing(self, b):
            return self.volt.at[:, pl.ds(0, 2), b + 1, body_rows, :]

        def direct(self, b):
            return pltpu.make_async_remote_copy(
                src_ref=self.leaving(b),
                dst_ref=self.landing(b),
                send_sem=self.send_sem.at[b],
                recv_sem=self.recv_sem.at[b],
                device_id=ahead,
                device_id_type=MESH_ID,
            )

        def to_relay(self, b):
            slot = self.number * relays + b
            return pltpu.make_async_remote_copy(
                src_ref=self.leaving(b),
                dst_ref=relayed.at[slot],
                send_sem=self.send_sem.at[b],
                recv_sem=relay_recv.at[slot],
                device_id=relay,
                device_id_type=MESH_ID,
            )

        def onward(self, b):
            slot = self.number * relays + b
            return pltpu.make_async_remote_copy(
                src_ref=relayed.at[slot],
                dst_ref=self.landing(b),
                send_sem=relay_send.at[slot],
                recv_sem=self.recv_sem.at[b],
                device_id=relay_target,
                device_id_type=MESH_ID,
            )

        def send(self, b):
            if has_relay:
                goes_round = is_source & (b < relays)
                pl.when(goes_round)(lambda: self.to_relay(b).start())
                pl.when(jnp.logical_not(goes_round))(lambda: self.direct(b).start())
            else:
                self.direct(b).start()

        def wait(self, b):
            self.direct(b).wait_recv()

        def wait_sent(self, b):
            self.direct(b).wait_send()

        def forward(self, low, high):
            if has_relay:

                @pl.when(is_relay)
                def _():
                    @pl.loop(low, high)
                    def _(b):
                        self.to_relay(b).wait_recv()
                        self.onward(b).start()

        def wait_forwarded(self):
            if has_relay:

                @pl.when(is_relay)
                def _():
                    @pl.loop(0, relays)
                    def _(b):
                        self.onward(b).wait_send()

    def start_leaving(b):
        lanes_b = pl.ds(pl.multiple_of(b * LANES, LANES), LANES)
        return volt_in.at[:, pl.ds(samples - 2, 2), :, lanes_b]

    def first_leaving(b):
        return first.at[:, pl.ds(samples, 2), b + 1, body_rows, :]

    before_one = Exchange(start, start_leaving, send_a, recv_a, 0)
    before_two = Exchange(first, first_leaving, send_b, recv_b, 1)

    def halo_copies(volt, low, count, slot):
        def one(row, to, device, sem):
            return pltpu.make_async_remote_copy(
                src_ref=volt.at[:, pl.ds(low + 2, count), pl.ds(1, blocks), pl.ds(row, 1), :],
                dst_ref=volt.at[:, pl.ds(low + 2, count), pl.ds(1, blocks), pl.ds(to, 1), :],
                send_sem=halo_send.at[sem],
                recv_sem=halo_recv.at[sem],
                device_id=device,
                device_id_type=MESH_ID,
            )

        up = one(TOP, TOP + rows, above, 2 * slot)
        down = one(TOP + rows - 1, TOP - 1, below, 2 * slot + 1)
        return up, down

    def send_halo(*what):
        up, down = halo_copies(*what)

        @pl.when(has_above)
        def _():
            up.start()

        @pl.when(has_below)
        def _():
            down.start()

    def wait_halo(*what):
        up, down = halo_copies(*what)

        @pl.when(has_below)
        def _():
            up.wait_recv()

        @pl.when(has_above)
        def _():
            down.wait_recv()

    def wait_halo_sent(*what):
        up, down = halo_copies(*what)

        @pl.when(has_above)
        def _():
            up.wait_send()

        @pl.when(has_below)
        def _():
            down.wait_send()

    pl.semaphore_wait(barrier, peers)

    early = jnp.where(is_source, relays, blocks // 4) if has_relay else blocks // 4
    pl.loop(0, early)(before_one.send)

    for copy in small[:3]:
        copy.wait()
    period = samples * slabs
    moments = slab * samples + lax.broadcasted_iota(jnp.int32, (samples, LANES), 0)
    row_ids = lax.broadcasted_iota(jnp.int32, (rows, LANES), 0)

    @pl.loop(0, cells // LANES)
    def _(k):
        nodes = node[pl.ds(k, 1), :]
        delay = moments - phase[pl.ds(k, 1), :]
        delay = jnp.where(delay < 0, delay + period, delay)
        weight = amp[pl.ds(k, 1), :] * jnp.where(
            delay < PULSE, (PULSE - delay).astype(F32) * (1.0 / PULSE), 0.0
        )
        high = weight.astype(BF).astype(F32)
        low = weight - high
        here = row_ids == lax.div(nodes, cols)
        place = pl.ds(pl.multiple_of(k * LANES, LANES), LANES)
        for s in range(samples):
            for part, value in ((0, high), (1, low)):
                spread[pl.ds((part * samples + s) * rows, rows), place] = jnp.where(
                    here, value[s : s + 1, :], 0.0
                ).astype(BF)
        x = lax.rem(nodes, cols).astype(F32)
        column[place, :] = jnp.broadcast_to(x, (LANES, LANES)).T

    wide = 2 * LANES
    lane_ids = lax.broadcasted_iota(jnp.int32, (1, LANES), 1).astype(F32)

    quads = blocks // 4

    @pl.loop(0, quads)
    def _(quad):
        for j in range(2):
            pair = quad * 2 + j
            base = (pair * wide).astype(F32)
            hot = jnp.concatenate(
                [
                    jnp.where(column[...] == lane_ids + (base + side * LANES), 1.0, 0.0).astype(BF)
                    for side in range(2)
                ],
                axis=1,
            )
            total = jnp.dot(spread[...], hot, preferred_element_type=F32)
            total = total[: samples * rows] + total[samples * rows :]
            for side in range(2):
                source[:, pair * 2 + side] = total[:, side * LANES : (side + 1) * LANES].reshape(
                    samples, rows, LANES
                )

        @pl.when(quad == 0)
        def _():
            @pl.loop(0, blocks)
            def _(b):
                load_block(b).wait()

            send_halo(start, 0, samples, 0)
            pl.loop(early, blocks)(before_one.send)

        @pl.when(quad > 0)
        def _():
            before_one.forward(2 * quad - 2, 2 * quad)

    for copy in small[3:]:
        copy.wait()

    @pl.loop(0, blocks)
    def _(b):
        for l in range(2):
            high, low = split(inverse[l, b])
            both = jnp.concatenate([high, low], axis=0)
            weights[l, b] = jnp.concatenate([both, both], axis=1)

    diag[...] = (1.5 * cap[...] + 2.0 * horiz[...]) + (2.0 * vert[...] + via[...][None])

    lanes = lax.broadcasted_iota(jnp.int32, (16, LANES), 1)
    is_first, is_last = lanes == 0, lanes == LANES - 1

    def sweep_block(volt, b, low, count):
        place = pl.ds(pl.multiple_of(b * LANES, LANES), LANES)
        highs = {}
        for h in range(rows // 16):
            strip = pl.ds(16 * h, 16)
            coef = [
                [ref[l, strip, place] for ref in (cap, horiz, vert, diag)] for l in range(2)
            ]
            via_h = via[strip, place]

            def load(l, s, shift=0, side=0):
                return volt[l, s + 2, b + 1 + side, pl.ds(TOP + 16 * h + shift, 16), :]

            for s in range(low, low + count):
                centre = [load(l, s) for l in range(2)]
                for l in range(2):
                    cap_h, horiz_h, vert_h, diag_h = coef[l]
                    mid = centre[l]
                    left = pltpu.roll(jnp.where(is_last, load(l, s, 0, -1), mid), 1, 1)
                    right = pltpu.roll(jnp.where(is_first, load(l, s, 0, 1), mid), LANES - 1, 1)
                    resid = (
                        cap_h * (2.0 * load(l, s - 1) - 0.5 * load(l, s - 2))
                        + horiz_h * (left + right)
                        + vert_h * (load(l, s, -1) + load(l, s, 1))
                        + (via_h * centre[1 - l] - diag_h * mid)
                    )
                    if l == 0:
                        resid = resid + source[s, b, strip, :]
                    highs[l, s, h] = split(resid)
        new = []
        for l in range(2):
            order = [(s, h) for s in range(low, low + count) for h in range(rows // 16)]
            left_side = jnp.concatenate(
                [
                    jnp.concatenate([highs[l, s, h][part] for s, h in order], axis=0)
                    for part in range(2)
                ],
                axis=1,
            )
            product = lax.dot_general(
                left_side, weights[l, b], (((1,), (1,)), ((), ())), preferred_element_type=F32
            )
            change = (product[:, :LANES] + product[:, LANES:]).reshape(count, rows, LANES)
            new.append(volt[l, pl.ds(low + 2, count), b + 1, body_rows, :] + change)
        return new

    unroll = 4
    turns = blocks // unroll

    def sweep(volt, low, count, store, before=None, after=None):
        @pl.loop(0, turns)
        def _(i):
            taken = [i * unroll + j for j in range(unroll)]
            if before is not None:
                for b in taken:
                    before(b)
            for b in taken:
                store(b, low, count, sweep_block(volt, b, low, count))
            if after is not None:
                after(i)

    def to_first(b, low, count, new):
        for l in range(2):
            first[l, pl.ds(low + 2, count), b + 1, body_rows, :] = new[l]

    def to_out(b, low, count, new):
        lanes_b = pl.ds(pl.multiple_of(b * LANES, LANES), LANES)
        for l in range(2):
            out[l, pl.ds(low, count), :, lanes_b] = new[l]

    last, middle = (samples - 2, 2), (2, samples - 4)

    def send_range(low, high):
        pl.loop(low, high)(before_two.send)

    def after_middle(i):
        pl.when(i == 1)(lambda: send_range(2, 4))

    def after_inner(i):
        pl.when(i < 3)(lambda: before_two.forward(3 + 2 * i, jnp.minimum(5 + 2 * i, relays)))

    def after_zero(i):
        pl.when(lax.rem(i, 2) == 1)(
            lambda: before_two.forward(lax.div(i, 2), lax.div(i, 2) + 1)
        )

    wait_halo(start, 0, samples, 0)
    sweep(start, *last, to_first)
    send_halo(first, *last, 1)
    send_range(0, 2)
    before_one.forward(2 * quads - 2, relays)
    sweep(start, *middle, to_first, after=after_middle)
    send_halo(first, *middle, 2)
    send_range(4, blocks // 2)
    sweep(start, 0, 2, to_first, before=before_one.wait, after=after_zero)
    send_halo(first, 0, 2, 3)
    send_range(blocks // 2, blocks)
    before_two.forward(2, 3)
    wait_halo(first, *last, 1)
    wait_halo(first, *middle, 2)
    sweep(first, 2, samples - 2, to_out, after=after_inner)
    wait_halo(first, 0, 2, 3)
    sweep(first, 0, 2, to_out, before=before_two.wait)

    @pl.loop(0, blocks)
    def _(b):
        before_one.wait_sent(b)
        before_two.wait_sent(b)

    before_one.wait_forwarded()
    before_two.wait_forwarded()
    wait_halo_sent(start, 0, samples, 0)
    wait_halo_sent(first, *last, 1)
    wait_halo_sent(first, *middle, 2)
    wait_halo_sent(first, 0, 2, 3)


def on_device(
    tiles,
    slabs,
    start_volt,
    cap_rate,
    horiz_cond,
    vert_cond,
    via_cond,
    line_inverse,
    cell_node,
    cell_phase,
    cell_amp,
):
    _, samples, rows, cols = start_volt.shape
    blocks = cols // LANES
    cells = cell_node.shape[0]
    grid = (2, samples + 2, blocks + 2, rows + 2 * TOP, LANES)
    dma = pltpu.SemaphoreType.DMA
    chunks = (cells // LANES, LANES)
    return pl.pallas_call(
        functools.partial(body, tiles, slabs),
        out_shape=pltpu.VMEM(start_volt.shape, F32),
        in_specs=[pl.BlockSpec(memory_space=pltpu.HBM)] * 9,
        out_specs=pl.BlockSpec(memory_space=pltpu.VMEM),
        scratch_shapes=[
            pltpu.VMEM(grid, F32),
            pltpu.VMEM(grid, F32),
            pltpu.VMEM(cap_rate.shape, F32),
            pltpu.VMEM(cap_rate.shape, F32),
            pltpu.VMEM(cap_rate.shape, F32),
            pltpu.VMEM(via_cond.shape, F32),
            pltpu.VMEM(cap_rate.shape, F32),
            pltpu.VMEM(line_inverse.shape, F32),
            pltpu.VMEM((2, blocks, 2 * LANES, 2 * LANES), BF),
            pltpu.VMEM((samples, blocks, rows, LANES), F32),
            pltpu.VMEM(chunks, jnp.int32),
            pltpu.VMEM(chunks, jnp.int32),
            pltpu.VMEM(chunks, F32),
            pltpu.VMEM((cells, LANES), F32),
            pltpu.VMEM((2 * samples * rows, cells), BF),
            dma((8,)),
            dma((blocks,)),
            dma((blocks,)),
            dma((blocks,)),
            dma((blocks,)),
            dma((blocks,)),
            dma((8,)),
            dma((8,)),
            pltpu.VMEM((blocks, 2, 2, rows, LANES), F32),
            dma((blocks,)),
            dma((blocks,)),
        ],
        compiler_params=pltpu.CompilerParams(
            collective_id=0, has_side_effects=True, vmem_limit_bytes=44 * 1024 * 1024
        ),
    )(
        *(
            pltpu.with_memory_space_constraint(value, pltpu.HBM)
            for value in (
                start_volt,
                cap_rate,
                horiz_cond,
                vert_cond,
                via_cond,
                line_inverse,
                cell_node.reshape(chunks),
                cell_phase.reshape(chunks),
                cell_amp.reshape(chunks),
            )
        )
    )


def solution(mesh):
    in_specs = (
        P(None, "slab", "tile", None),
        P(None, "tile", None),
        P(None, "tile", None),
        P(None, "tile", None),
        P("tile", None),
        P(),
        P("tile"),
        P("tile"),
        P("tile"),
    )
    out_specs = P(None, "slab", "tile", None)
    return jax.shard_map(
        functools.partial(on_device, mesh.shape["tile"], mesh.shape["slab"]),
        mesh=mesh,
        in_specs=in_specs,
        out_specs=out_specs,
        check_vma=False,
    )
```
